512 devices in a mesh: section: 16 (over x, y), row: 4 (over z_hi, core), col: 8 (over z_lo).
Axes of the slice: x: 4, y: 4, z: 16 (z_hi: 2, z_lo: 8; z = z_hi * 8 + z_lo), core: 2. Of those that a mesh axis runs over, the one named last changes fastest.
Arguments:
- inputs: bfloat16 [16, 3, 128, 2048], P('section', None, 'row', 'col'), may hold values from -6 to 6
- sample_ids: int32 [18], replicated, may hold values from 0 to 15
- send_base: bfloat16 [16, 16, 128, 2048], P('section', None, 'row', 'col'), may hold values from -1.796875 to 1.796875
- recv_base: bfloat16 [16, 16, 128, 2048], P('section', None, 'row', 'col'), may hold values from -1.796875 to 1.796875
- w_up: bfloat16 [16, 2048, 8192], P('section', 'col', 'row'), may hold values from -0.125 to 0.125
- w_down: bfloat16 [16, 8192, 2048], P('section', 'row', 'col'), may hold values from -0.0625 to 0.0625
- cotangent: bfloat16 [16, 3, 128, 2048], P('section', None, 'row', 'col'), may hold values from -6 to 6
Outputs:
- section_input: bfloat16 [16, 3, 128, 2048], P('section', None, 'row', 'col')
- section_output: bfloat16 [16, 3, 128, 2048], P('section', None, 'row', 'col')
- input_grad: bfloat16 [16, 3, 128, 2048], P('section', None, 'row', 'col')
- grad_up: bfloat16 [16, 2048, 8192], P('section', 'col', 'row')
- grad_down: bfloat16 [16, 8192, 2048], P('section', 'row', 'col')
The draws below stay inside these ranges and needn't reach their ends.
All inputs are finite; a program needn't handle non-finite values.
Results may differ from the reference program's by a relative error of at most 0.04.
Values may be sent and summed in bfloat16 or wider, within the bound.
A program may use at most 64 MiB of HBM per device.

```python
import jax
import jax.numpy as jnp
from jax import lax

D = 2048
FF = 8192
MTOK = 128
TICKS = 3
SAMPLES = 16
N_SECTION = 16
N_ROW = 4
N_COL = 8


def set_ends(entries, rng, smallest, high):
    place = [jax.random.randint(jax.random.fold_in(rng, axis), (), 0, length) for axis, length in enumerate(entries.shape)]
    main_axis = entries.shape.index(max(entries.shape))
    beside = place[:main_axis] + [(place[main_axis] + 1) % entries.shape[main_axis]] + place[main_axis + 1:]
    return entries.at[tuple(place)].set(smallest).at[tuple(beside)].set(high)


def steps_of(own_key, shape, cuts, low, high):
    level = 1.0
    for dim, shards_of in cuts:
        draws = jax.random.uniform(jax.random.fold_in(jax.random.fold_in(own_key, 6), dim), (shards_of,), jnp.float32, low / len(cuts), high / len(cuts))
        level = level * jnp.repeat(jnp.exp(draws), shape[dim] // shards_of).reshape((-1,) + (1,) * (len(shape) - 1 - dim))
    return level


def noise(stream_key, dims, scale, limit, pieces=(), kind=jnp.bfloat16):
    array = scale * jax.random.normal(stream_key, dims, jnp.float32)
    if pieces:
        array = array * steps_of(stream_key, dims, pieces, -0.22, 0.18)
    return jnp.clip(array, -limit, limit).astype(kind)


def setup_inputs(seed: int = 0) -> dict:
    splits = jax.random.split(jax.random.key(seed), 8)
    return {
        "inputs": noise(splits[0], (N_SECTION, TICKS, MTOK, D), 1.0, 6.0, ((0, 16), (2, 4), (3, 8))),
        "sample_ids": set_ends(jax.random.randint(splits[1], (N_SECTION + TICKS - 1,), 0, SAMPLES), jax.random.fold_in(splits[1], 1), 0, SAMPLES - 1).astype(jnp.int32),
        "send_base": noise(splits[2], (N_SECTION, SAMPLES, MTOK, D), 0.3, 1.796875, ((0, 16), (2, 4), (3, 8))),
        "recv_base": noise(splits[3], (N_SECTION, SAMPLES, MTOK, D), 0.3, 1.796875, ((0, 16), (2, 4), (3, 8))),
        "w_up": noise(splits[4], (N_SECTION, D, FF), D ** -0.5, 0.125, ((0, 16), (1, 8), (2, 4))),
        "w_down": noise(splits[5], (N_SECTION, FF, D), FF ** -0.5, 0.0625, ((0, 16), (1, 4), (2, 8))),
        "cotangent": noise(splits[6], (N_SECTION, TICKS, MTOK, D), 1.0, 6.0, ((0, 16), (2, 4), (3, 8))),
    }


def split_sum(left, right, parts):
    size = left.shape[1] // parts
    total = jnp.zeros((left.shape[0], right.shape[1]), jnp.float32)
    for index in range(parts):
        block = jnp.dot(left[:, index * size:(index + 1) * size], right[index * size:(index + 1) * size], preferred_element_type=jnp.float32)
        total = total + lax.optimization_barrier(block.astype(jnp.bfloat16)).astype(jnp.float32)
    return total


def silu_slope(value):
    sig = jax.nn.sigmoid(value)
    return sig * (1.0 + value * (1.0 - sig))


def reference(inputs, sample_ids, send_base, recv_base, w_up, w_down, cotangent):
    entering = [[None] * TICKS for index in range(N_SECTION)]
    leaving = [[None] * TICKS for index in range(N_SECTION)]
    deltas = [[None] * TICKS for index in range(N_SECTION)]
    hidden_pre = [[None] * TICKS for index in range(N_SECTION)]
    hidden_act = [[None] * TICKS for index in range(N_SECTION)]
    for tick in range(TICKS):
        for section in range(N_SECTION):
            sample = sample_ids[tick - section + N_SECTION - 1]
            if tick == 0 or section == 0:
                current = inputs[section, tick]
            else:
                stored = lax.dynamic_index_in_dim(recv_base[section], sample, 0, keepdims=False)
                current = (stored.astype(jnp.float32) + deltas[section - 1][tick - 1].astype(jnp.float32)).astype(jnp.bfloat16)
            entering[section][tick] = current
            pre = split_sum(current, w_up[section], N_COL)
            act = jax.nn.silu(pre).astype(jnp.bfloat16)
            output = (current.astype(jnp.float32) + split_sum(act, w_down[section], N_ROW)).astype(jnp.bfloat16)
            hidden_pre[section][tick] = pre
            hidden_act[section][tick] = act
            leaving[section][tick] = output
            sent = lax.dynamic_index_in_dim(send_base[section], sample, 0, keepdims=False)
            deltas[section][tick] = (output.astype(jnp.float32) - sent.astype(jnp.float32)).astype(jnp.bfloat16)
    back = [[None] * TICKS for index in range(N_SECTION)]
    total_up = [jnp.zeros((D, FF), jnp.float32) for index in range(N_SECTION)]
    total_down = [jnp.zeros((FF, D), jnp.float32) for index in range(N_SECTION)]
    for turn in range(TICKS):
        tick = TICKS - 1 - turn
        for section in range(N_SECTION - 1, -1, -1):
            if turn == 0 or section == N_SECTION - 1:
                grad_out = cotangent[section, tick]
            else:
                grad_out = back[section + 1][tick + 1]
            grad_act = split_sum(grad_out, w_down[section].T, N_COL)
            grad_pre = (grad_act * silu_slope(hidden_pre[section][tick])).astype(jnp.bfloat16)
            grad_in = (grad_out.astype(jnp.float32) + split_sum(grad_pre, w_up[section].T, N_ROW)).astype(jnp.bfloat16)
            back[section][tick] = grad_in
            total_up[section] = total_up[section] + jnp.dot(entering[section][tick].T, grad_pre, preferred_element_type=jnp.float32)
            total_down[section] = total_down[section] + jnp.dot(hidden_act[section][tick].T, grad_out, preferred_element_type=jnp.float32)
    section_input = jnp.stack([jnp.stack(entering[index]) for index in range(N_SECTION)])
    section_output = jnp.stack([jnp.stack(leaving[index]) for index in range(N_SECTION)])
    input_grad = jnp.stack([jnp.stack(back[index]) for index in range(N_SECTION)])
    grads_up = jnp.stack([value.astype(jnp.bfloat16) for value in total_up])
    grads_down = jnp.stack([value.astype(jnp.bfloat16) for value in total_down])
    return (section_input, section_output, input_grad, grads_up, grads_down)
```

```python
import jax
import jax.numpy as jnp
from jax import lax
from jax.experimental import pallas as pl
from jax.experimental.pallas import tpu as pltpu
from jax.sharding import PartitionSpec as P

MESH = pl.DeviceIdType.MESH
GROUP = 4
F32 = jnp.float32
BF16 = jnp.bfloat16


def sigmoid(value):
    return 1.0 / (1.0 + jnp.exp(-value))


def kernel(
    ids, inputs, send_base, recv_base, w_up, w_down, cotangent,
    sec_in, sec_out, in_grad, grad_up, grad_down,
    xs, gs, stage, base, late, act, gpre, pre, gsum,
    a_out, a_in, b_out, b_in, part, swap_in, p_out, relay_in, own_in,
    pre_send, pre_recv, a_send, a_recv, b_send, b_recv, c_send, c_recv,
    s_send, s_recv, r_send, r_recv, o_send, o_recv,
):
    ticks, rows, width = inputs.shape
    tokens = xs.shape[0] // ticks
    chunks = tokens // rows
    half = rows // 2
    shard = act.shape[2]
    section, row, col = (lax.axis_index(n) for n in ("section", "row", "col"))
    sections, n_row, n_col = (lax.axis_size(n) for n in ("section", "row", "col"))
    core = lax.rem(row, 2)
    place = lax.rem(col, GROUP)
    first = col - place
    mates = [{"col": first + lax.rem(place + d, GROUP)} for d in range(1, GROUP)]
    across = {"col": lax.rem(col + GROUP, n_col)}
    peers = [{"row": lax.rem(row + d, n_row)} for d in range(1, n_row)]
    twin = {"row": row + 1 - 2 * core}
    ahead = lax.rem(section + 1, sections)
    behind = lax.rem(section + sections - 1, sections)
    ahead_ids = [{"section": ahead, "row": lax.rem(row + d, n_row)} for d in range(n_row)]
    behind_ids = [{"section": behind, "row": lax.rem(row + d, n_row)} for d in range(n_row)]

    def remote(src, dst, send_sem, recv_sem, where):
        pltpu.make_async_remote_copy(
            src_ref=src, dst_ref=dst, send_sem=send_sem, recv_sem=recv_sem,
            device_id=where, device_id_type=MESH,
        ).start()

    def await_bytes(ref, sem):
        pltpu.make_async_copy(ref, ref, sem).wait()

    def chunk_rows(tick, chunk):
        return pl.ds(pl.multiple_of(tick * tokens + chunk * rows, rows), rows)

    def own_rows(tick):
        return chunk_rows(tick, row)

    def pick(table, tick):
        return table[ids[tick - section + sections - 1]]

    def each(task):
        def body(chunk, carry):
            task(chunk)
            return carry

        lax.fori_loop(0, chunks, body, 0)

    barrier = pltpu.get_barrier_semaphore()
    friends = mates + [across] + peers + ahead_ids + behind_ids
    for friend in friends:
        pl.semaphore_signal(barrier, inc=1, device_id=friend, device_id_type=MESH)
    pl.semaphore_wait(barrier, len(friends))

    for peer in peers:
        remote(inputs.at[0], xs.at[own_rows(0)], pre_send.at[0], pre_recv.at[0], peer)
    for tick in range(1, ticks):
        stage[tick - 1] = jnp.where(section == 0, inputs[tick], pick(recv_base, tick))
    for peer in peers:
        remote(cotangent.at[ticks - 1], gs.at[own_rows(ticks - 1)], pre_send.at[1], pre_recv.at[1], peer)
    for peer in peers:
        for tick in range(1, ticks):
            remote(stage.at[tick - 1], base.at[tick - 1, pl.ds(row * rows, rows)], pre_send.at[2], pre_recv.at[2], peer)
    last = section == sections - 1

    @pl.when(last)
    def _():
        for peer in peers:
            for tick in range(ticks - 1):
                remote(cotangent.at[tick], late.at[tick, pl.ds(row * rows, rows)], pre_send.at[3], pre_recv.at[3], peer)

    xs[own_rows(0), :] = inputs[0]
    gs[own_rows(ticks - 1), :] = cotangent[ticks - 1]
    for tick in range(1, ticks):
        base[tick - 1, pl.ds(pl.multiple_of(row * rows, rows), rows), :] = stage[tick - 1]
    for tick in range(ticks - 1):
        late[tick, pl.ds(pl.multiple_of(row * rows, rows), rows), :] = cotangent[tick]

    def expand(phase, tick, source, weight):
        def task(chunk):
            value = source[chunk_rows(tick, chunk), :]
            for d in (1, 2, 3, 0):
                columns = pl.ds(pl.multiple_of(lax.rem(place + d, GROUP) * shard, shard), shard)
                a_out[phase, chunk, d] = weight(value, columns).astype(BF16)
                if d:
                    remote(a_out.at[phase, chunk, d], a_in.at[phase, chunk, d - 1], a_send.at[phase], a_recv.at[phase, chunk], mates[d - 1])

        return task

    def up(value, columns):
        return jnp.dot(value, w_up[:, columns], preferred_element_type=F32)

    def down_t(value, columns):
        return lax.dot_general(value, w_down[columns, :], (((1,), (1,)), ((), ())), preferred_element_type=F32)

    def combine(phase):
        def task(chunk):
            await_bytes(a_in.at[phase, chunk], a_recv.at[phase, chunk])
            total = a_out[phase, chunk, 0].astype(F32)
            for d in range(GROUP - 1):
                total = total + a_in[phase, chunk, d].astype(F32)
            b_out[phase, chunk] = total.astype(BF16)
            remote(b_out.at[phase, chunk], b_in.at[phase, chunk], b_send.at[phase], b_recv.at[phase, chunk], across)

        return task

    def summed(phase, chunk):
        await_bytes(b_in.at[phase, chunk], b_recv.at[phase, chunk])
        return b_out[phase, chunk].astype(F32) + b_in[phase, chunk].astype(F32)

    def spread(phase, tick, chunk, hidden):
        for mate in mates:
            ref = hidden.at[place, chunk_rows(tick, chunk)]
            remote(ref, ref, c_send.at[phase], c_recv.at[phase, chunk], mate)

    def activate(phase, tick):
        def task(chunk):
            value = summed(phase, chunk)
            pre[chunk_rows(tick, chunk), :] = value
            act[place, chunk_rows(tick, chunk), :] = (value * sigmoid(value)).astype(BF16)
            spread(phase, tick, chunk, act)

        return task

    def slope(value):
        sig = sigmoid(value)
        return sig * (1.0 + value * (1.0 - sig))

    def differentiate(phase, tick):
        def task(chunk):
            value = summed(phase, chunk) * slope(pre[chunk_rows(tick, chunk), :])
            gpre[place, chunk_rows(tick, chunk), :] = value.astype(BF16)
            spread(phase, tick, chunk, gpre)

        return task

    def contract(phase, tick, hidden, weight, skip):
        def task(chunk):
            await_bytes(hidden.at[pl.ds(0, GROUP - 1), chunk_rows(tick, chunk)], c_recv.at[phase, chunk])
            total = jnp.where(row == chunk, skip(), 0.0)
            for j in range(GROUP):
                total = total + weight(hidden[j, chunk_rows(tick, chunk), :], pl.ds(j * shard, shard))
            part[phase, chunk, 0] = total[:half]
            part[phase, chunk, 1] = total[half:]
            remote(part.at[phase, chunk, 1 - core], swap_in.at[phase, chunk], s_send.at[phase], s_recv.at[phase, chunk], twin)

        return task

    def down(value, columns):
        return jnp.dot(value, w_down[columns, :], preferred_element_type=F32)

    def up_t(value, columns):
        return lax.dot_general(value, w_up[:, columns], (((1,), (1,)), ((), ())), preferred_element_type=F32)

    def forward_skip(tick):
        return lambda: xs[own_rows(tick), :].astype(F32) - pick(send_base, tick).astype(F32)

    def backward_skip(tick):
        return lambda: gs[own_rows(tick), :].astype(F32)

    def hand_on(phase, targets):
        def task(chunk):
            await_bytes(swap_in.at[phase, chunk], s_recv.at[phase, chunk])
            total = part[phase, chunk, core] + swap_in[phase, chunk]
            p_out[phase, chunk] = total.astype(BF16)
            for target in targets:
                remote(p_out.at[phase, chunk], relay_in.at[phase, chunk, row], r_send.at[phase], r_recv.at[phase, chunk], target)

            @pl.when(row == chunk)
            def _():
                own_in[phase, row] = p_out[phase, chunk]

            @pl.when(row != chunk)
            def _():
                remote(p_out.at[phase, chunk], own_in.at[phase, row], o_send.at[phase], o_recv.at[phase], {"row": chunk})

        return task

    def halves(ref):
        low = ref[0].astype(F32) + ref[2].astype(F32)
        high = ref[1].astype(F32) + ref[3].astype(F32)
        return jnp.concatenate([low, high], axis=0)

    def enter(phase, tick):
        def task(chunk):
            await_bytes(relay_in.at[phase, chunk], r_recv.at[phase, chunk])
            here = base[tick - 1, pl.ds(pl.multiple_of(chunk * rows, rows), rows), :]
            rebuilt = (here.astype(F32) + halves(relay_in.at[phase, chunk])).astype(BF16)
            xs[chunk_rows(tick, chunk), :] = jnp.where(section == 0, here, rebuilt)

        return task

    def enter_back(phase, tick):
        def task(chunk):
            await_bytes(relay_in.at[phase, chunk], r_recv.at[phase, chunk])
            here = late[tick, pl.ds(pl.multiple_of(chunk * rows, rows), rows), :]
            arrived = halves(relay_in.at[phase, chunk]).astype(BF16)
            gs[chunk_rows(tick, chunk), :] = jnp.where(last, here, arrived)

        return task

    def both(one, two):
        def task(chunk):
            one(chunk)
            two(chunk)

        return task

    def own_sum(phase):
        await_bytes(own_in.at[phase, pl.ds(0, n_row - 1)], o_recv.at[phase])
        return halves(own_in.at[phase])

    def keep_output(tick):
        sec_in[tick] = xs[own_rows(tick), :]
        sec_out[tick] = (own_sum(tick) + pick(send_base, tick).astype(F32)).astype(BF16)

    def keep_grad(tick):
        in_grad[tick] = own_sum(ticks + tick).astype(BF16)

    top = ticks - 1
    back = ticks + top
    await_bytes(xs.at[pl.ds(0, (n_row - 1) * rows)], pre_recv.at[0])
    for tick in range(ticks):
        step = expand(tick, tick, xs, up)
        if tick:
            step = both(enter(tick - 1, tick), step)
        each(step)
        each(combine(tick))
        if tick < top:
            each(activate(tick, tick))
            each(contract(tick, tick, act, down, forward_skip(tick)))
            each(hand_on(tick, ahead_ids))
        if tick == 0:
            await_bytes(gs.at[pl.ds(0, (n_row - 1) * rows)], pre_recv.at[1])
            await_bytes(base.at[:, pl.ds(0, (n_row - 1) * rows)], pre_recv.at[2])

            @pl.when(last)
            def _():
                await_bytes(late.at[:, pl.ds(0, (n_row - 1) * rows)], pre_recv.at[3])

            each(expand(back, top, gs, down_t))
        if tick == 1:
            each(combine(back))
            keep_output(0)
    each(both(activate(top, top), differentiate(back, top)))
    each(contract(back, top, gpre, up_t, backward_skip(top)))
    each(hand_on(back, behind_ids))
    each(contract(top, top, act, down, forward_skip(top)))
    each(hand_on(top, []))
    keep_output(1)
    for tick in range(top - 1, -1, -1):
        phase = ticks + tick
        each(both(enter_back(phase + 1, tick), expand(phase, tick, gs, down_t)))
        if tick == top - 1:
            keep_output(top)
        each(combine(phase))
        each(differentiate(phase, tick))
        each(contract(phase, tick, gpre, up_t, backward_skip(tick)))
        each(hand_on(phase, behind_ids if tick else []))
        keep_grad(tick + 1)

    contract_first = (((0,), (0,)), ((), ()))
    for j in range(GROUP):
        columns = pl.ds(j * shard, shard)
        grad_up[:, columns] = lax.dot_general(xs[...], gpre[j], contract_first, preferred_element_type=F32).astype(BF16)
        grad_down[columns, :] = lax.dot_general(act[j], gs[...], contract_first, preferred_element_type=F32).astype(BF16)
    keep_grad(0)

    count = (n_row - 1) * rows
    await_bytes(xs.at[pl.ds(0, count)], pre_send.at[0])
    await_bytes(gs.at[pl.ds(0, count)], pre_send.at[1])
    await_bytes(base.at[:, pl.ds(0, count)], pre_send.at[2])

    @pl.when(last)
    def _():
        await_bytes(late.at[:, pl.ds(0, count)], pre_send.at[3])

    for phase in range(2 * ticks):
        await_bytes(a_in.at[phase], a_send.at[phase])
        await_bytes(b_in.at[phase], b_send.at[phase])
        await_bytes(act.at[pl.ds(0, GROUP - 1), pl.ds(0, tokens)], c_send.at[phase])
        await_bytes(swap_in.at[phase], s_send.at[phase])
        if phase != top and phase != ticks:
            await_bytes(relay_in.at[phase], r_send.at[phase])
        await_bytes(own_in.at[phase, pl.ds(0, n_row - 1)], o_send.at[phase])


def per_device(inputs, sample_ids, send_base, recv_base, w_up, w_down, cotangent):
    ticks, rows, width = inputs.shape[1:]
    chunks = lax.axis_size("row")
    tokens = rows * chunks
    hidden = w_up.shape[2]
    shard = hidden // GROUP
    phases = 2 * ticks
    half = rows // 2
    dma = pltpu.SemaphoreType.DMA
    vmem = pl.BlockSpec(memory_space=pltpu.VMEM)
    outs = pl.pallas_call(
        kernel,
        out_shape=[
            jax.ShapeDtypeStruct((ticks, rows, width), BF16),
            jax.ShapeDtypeStruct((ticks, rows, width), BF16),
            jax.ShapeDtypeStruct((ticks, rows, width), BF16),
            jax.ShapeDtypeStruct((width, hidden), BF16),
            jax.ShapeDtypeStruct((hidden, width), BF16),
        ],
        in_specs=[pl.BlockSpec(memory_space=pltpu.SMEM)] + [vmem] * 6,
        out_specs=[vmem] * 5,
        scratch_shapes=[
            pltpu.VMEM((ticks * tokens, width), BF16),
            pltpu.VMEM((ticks * tokens, width), BF16),
            pltpu.VMEM((ticks - 1, rows, width), BF16),
            pltpu.VMEM((ticks - 1, tokens, width), BF16),
            pltpu.VMEM((ticks - 1, tokens, width), BF16),
            pltpu.VMEM((GROUP, ticks * tokens, shard), BF16),
            pltpu.VMEM((GROUP, ticks * tokens, shard), BF16),
            pltpu.VMEM((ticks * tokens, shard), F32),
            pltpu.VMEM((8, 128), F32),
            pltpu.VMEM((phases, chunks, GROUP, rows, shard), BF16),
            pltpu.VMEM((phases, chunks, GROUP - 1, rows, shard), BF16),
            pltpu.VMEM((phases, chunks, rows, shard), BF16),
            pltpu.VMEM((phases, chunks, rows, shard), BF16),
            pltpu.VMEM((phases, chunks, 2, half, width), F32),
            pltpu.VMEM((phases, chunks, half, width), F32),
            pltpu.VMEM((phases, chunks, half, width), BF16),
            pltpu.VMEM((phases, chunks, chunks, half, width), BF16),
            pltpu.VMEM((phases, chunks, half, width), BF16),
            dma((4,)), dma((4,)),
            dma((phases,)), dma((phases, chunks)),
            dma((phases,)), dma((phases, chunks)),
            dma((phases,)), dma((phases, chunks)),
            dma((phases,)), dma((phases, chunks)),
            dma((phases,)), dma((phases, chunks)),
            dma((phases,)), dma((phases,)),
        ],
        compiler_params=pltpu.CompilerParams(
            collective_id=0, has_side_effects=True, vmem_limit_bytes=56 << 20
        ),
    )(sample_ids, inputs[0], send_base[0], recv_base[0], w_up[0], w_down[0], cotangent[0])
    return tuple(value[None] for value in outs)


def solution(mesh):
    pieces = P("section", None, "row", "col")
    ups, downs = P("section", "col", "row"), P("section", "row", "col")
    return jax.shard_map(
        per_device,
        mesh=mesh,
        in_specs=(pieces, P(), pieces, pieces, ups, downs, pieces),
        out_specs=(pieces, pieces, pieces, ups, downs),
        check_vma=False,
    )
```

```python
import jax
import jax.numpy as jnp
from jax import lax
from jax.experimental import pallas as pl
from jax.experimental.pallas import tpu as pltpu
from jax.sharding import PartitionSpec as P

MESH = pl.DeviceIdType.MESH
GROUP = 4
SIZE = 16
PERIOD = 34
STRIDE = 3
AT_COMBINE, AT_GATHER, AT_ACTIVATE, AT_FORWARD, AT_CONTRACT, AT_HAND = 4, 9, 14, 19, 25, 26
EARLY_START, EARLY_EVERY = 19, 3
SPARE_START, SPARE_EVERY = 106, 3
F32 = jnp.float32
BF16 = jnp.bfloat16


def kernel(
    ids, inputs, send_base, recv_base, w_up, w_down, cotangent,
    sec_in, sec_out, in_grad, grad_up, grad_down,
    up_t, down_t, xs, gs, stage, base, late, act, gpre, pre,
    a_out, a_in, c_out, b_out, b_in, part, swap_in, p_out, relay_in, own_in,
    pre_send, pre_recv, a_send, a_recv, b_send, b_recv, c_send, c_recv,
    s_send, s_recv, r_send, r_recv, o_send, o_recv,
):
    ticks, rows, width = inputs.shape
    tokens = xs.shape[0] // ticks
    chunks, size, wide = a_out.shape[1], a_out.shape[3], a_out.shape[4]
    per_row = rows // size
    half = width // 2
    top = ticks - 1
    phases = 2 * ticks
    section, row, col = (lax.axis_index(n) for n in ("section", "row", "col"))
    sections, n_row, n_col = (lax.axis_size(n) for n in ("section", "row", "col"))
    core = lax.rem(row, 2)
    place = lax.rem(col, GROUP)
    first = col - place
    rank = jnp.where(first == 0, GROUP - 1 - place, place)

    def at_rank(number):
        return {"col": first + jnp.where(first == 0, GROUP - 1 - number, number)}

    mates = [{"col": first + lax.rem(place + d, GROUP)} for d in range(1, GROUP)]
    across = {"col": n_col - 1 - col}
    peers = [{"row": lax.rem(row + d, n_row)} for d in range(1, n_row)]
    twin = {"row": row + 1 - 2 * core}
    ahead = lax.rem(section + 1, sections)
    behind = lax.rem(section + sections - 1, sections)
    ahead_ids = [{"section": ahead, "row": lax.rem(row + d, n_row)} for d in range(n_row)]
    behind_ids = [{"section": behind, "row": lax.rem(row + d, n_row)} for d in range(n_row)]

    def remote(src, dst, send_sem, recv_sem, where):
        pltpu.make_async_remote_copy(
            src_ref=src, dst_ref=dst, send_sem=send_sem, recv_sem=recv_sem,
            device_id=where, device_id_type=MESH,
        ).start()

    def await_bytes(ref, sem):
        pltpu.make_async_copy(ref, ref, sem).wait()

    def span(start, count):
        return pl.ds(pl.multiple_of(start, count), count)

    def chunk_rows(tick, chunk):
        return span(tick * tokens + chunk * size, size)

    def own_rows(tick):
        return span(tick * tokens + row * rows, rows)

    def pick(table, tick):
        return table[ids[tick - section + sections - 1]]

    barrier = pltpu.get_barrier_semaphore()
    friends = mates + [across] + peers + ahead_ids + behind_ids
    for friend in friends:
        pl.semaphore_signal(barrier, inc=1, device_id=friend, device_id_type=MESH)
    pl.semaphore_wait(barrier, len(friends))

    last = section == sections - 1
    for peer in peers:
        remote(inputs.at[0], xs.at[own_rows(0)], pre_send.at[0], pre_recv.at[0], peer)
    for tick in range(1, ticks):
        stage[tick - 1] = jnp.where(section == 0, inputs[tick], pick(recv_base, tick))
    for peer in peers:
        remote(cotangent.at[top], gs.at[own_rows(top)], pre_send.at[1], pre_recv.at[1], peer)
    for peer in peers:
        for tick in range(1, ticks):
            remote(stage.at[tick - 1], base.at[tick - 1, span(row * rows, rows)], pre_send.at[2], pre_recv.at[2], peer)

    @pl.when(last)
    def _():
        for peer in peers:
            for tick in range(top):
                remote(cotangent.at[tick], late.at[tick, span(row * rows, rows)], pre_send.at[3], pre_recv.at[3], peer)

    xs[own_rows(0), :] = inputs[0]
    gs[own_rows(top), :] = cotangent[top]
    for tick in range(1, ticks):
        base[tick - 1, span(row * rows, rows), :] = stage[tick - 1]
    for tick in range(top):
        late[tick, span(row * rows, rows), :] = cotangent[tick]

    early_half = jnp.where(rank >= 2, 1, 0)
    early_to = at_rank(jnp.where(rank == 1, 0, 1))
    early_slot = jnp.where(rank == 3, 0, 1)

    def expand(phase, chunk, value, product):
        def compute(side):
            a_out[phase, chunk, side] = product(value, span(side * wide, wide)).astype(BF16)

        compute(early_half)

        @pl.when(rank > 0)
        def _():
            remote(a_out.at[phase, chunk, early_half], a_in.at[phase, chunk, early_slot], a_send.at[phase], a_recv.at[phase, chunk], early_to)

        compute(1 - early_half)

        @pl.when(rank == 3)
        def _():
            remote(a_out.at[phase, chunk, 0], a_in.at[phase, chunk, 0], a_send.at[phase], a_recv.at[phase, chunk], at_rank(2))

    def expand_forward(tick, chunk):
        def product(value, columns):
            return jnp.dot(value, w_up[:, columns], preferred_element_type=F32)

        expand(tick, chunk, xs[chunk_rows(tick, chunk), :], product)

    def expand_back(tick, chunk):
        def product(value, columns):
            return jnp.dot(value, down_t[:, columns], preferred_element_type=F32)

        expand(ticks + tick, chunk, gs[chunk_rows(tick, chunk), :], product)

    def partial_sum(phase, chunk, side, slots):
        total = a_out[phase, chunk, side].astype(F32)
        for slot in slots:
            total = total + a_in[phase, chunk, slot].astype(F32)
        return total.astype(BF16)

    def combine(phase, chunk):
        def pass_on(side, slots, slot):
            await_bytes(a_in.at[phase, chunk, pl.ds(0, slots)], a_recv.at[phase, chunk])
            c_out[phase, chunk] = partial_sum(phase, chunk, side, range(slots))
            remote(c_out.at[phase, chunk], a_in.at[phase, chunk, slot], a_send.at[phase], a_recv.at[phase, chunk], at_rank(0))

        @pl.when(rank == 2)
        def _():
            pass_on(0, 1, 0)

        @pl.when(rank == 1)
        def _():
            pass_on(1, 2, 2)

    def gather(phase, chunk):
        await_bytes(a_in.at[phase, chunk], a_recv.at[phase, chunk])
        b_out[phase, chunk, 0] = partial_sum(phase, chunk, 0, (0, 1))
        b_out[phase, chunk, 1] = partial_sum(phase, chunk, 1, (2,))
        remote(b_out.at[phase, chunk], b_in.at[phase, chunk], b_send.at[phase], b_recv.at[phase, chunk], across)

    def summed(phase, chunk):
        await_bytes(b_in.at[phase, chunk], b_recv.at[phase, chunk])
        return b_out[phase, chunk].astype(F32) + b_in[phase, chunk].astype(F32)

    def spread(phase, tick, chunk, hidden):
        def send(side, number):
            ref = hidden.at[side, chunk_rows(tick, chunk)]
            remote(ref, ref, c_send.at[phase], c_recv.at[phase, chunk, side], at_rank(number))

        send(1, 1)
        send(0, 2)
        send(0, 1)

    def forward(phase, tick, chunk, hidden):
        def pass_on(side, numbers):
            ref = hidden.at[side, chunk_rows(tick, chunk)]
            await_bytes(ref, c_recv.at[phase, chunk, side])
            for number in numbers:
                remote(ref, ref, c_send.at[phase], c_recv.at[phase, chunk, side], at_rank(number))

        @pl.when(rank == 1)
        def _():
            pass_on(1, (3, 2))

        @pl.when(rank == 2)
        def _():
            pass_on(0, (3,))

    def activate(tick, chunk):
        value = summed(tick, chunk)
        pre[:, chunk_rows(tick, chunk), :] = value
        act[:, chunk_rows(tick, chunk), :] = (value / (1.0 + jnp.exp(-value))).astype(BF16)

    def differentiate(tick, chunk):
        value = pre[:, chunk_rows(tick, chunk), :]
        sig = 1.0 / (1.0 + jnp.exp(-value))
        slope = sig * (1.0 + value * (1.0 - sig))
        gpre[:, chunk_rows(tick, chunk), :] = (summed(ticks + tick, chunk) * slope).astype(BF16)
        spread(ticks + tick, tick, chunk, gpre)

    def await_hidden(phase, tick, chunk, hidden):
        for side, known in ((0, 2), (1, 1)):
            @pl.when(jnp.logical_and(rank != 0, rank != known))
            def _(side=side):
                await_bytes(hidden.at[side, chunk_rows(tick, chunk)], c_recv.at[phase, chunk, side])

    def swap(phase, chunk, total, skip):
        def halves(value):
            return value[:, :half], value[:, half:]

        part[phase, chunk, 0], part[phase, chunk, 1] = halves(total)

        @pl.when(row == lax.div(chunk, per_row))
        def _():
            part[phase, chunk, 0], part[phase, chunk, 1] = halves(total + skip())

        remote(part.at[phase, chunk, 1 - core], swap_in.at[phase, chunk], s_send.at[phase], s_recv.at[phase, chunk], twin)

    def contract_forward(tick, chunk):
        await_hidden(tick, tick, chunk, act)
        total = 0.0
        for side in range(2):
            total = total + jnp.dot(act[side, chunk_rows(tick, chunk), :], w_down[pl.ds(side * wide, wide), :], preferred_element_type=F32)

        def skip():
            sample = ids[tick - section + sections - 1]
            stored = send_base[sample, span(lax.rem(chunk, per_row) * size, size), :]
            return xs[chunk_rows(tick, chunk), :].astype(F32) - stored.astype(F32)

        swap(tick, chunk, total, skip)

    def contract_back(tick, chunk):
        await_hidden(ticks + tick, tick, chunk, gpre)
        total = 0.0
        for side in range(2):
            total = total + jnp.dot(gpre[side, chunk_rows(tick, chunk), :], up_t[pl.ds(side * wide, wide), :], preferred_element_type=F32)
        swap(ticks + tick, chunk, total, lambda: gs[chunk_rows(tick, chunk), :].astype(F32))

    def hand_on(phase, chunk):
        await_bytes(swap_in.at[phase, chunk], s_recv.at[phase, chunk])
        p_out[phase, chunk] = (part[phase, chunk, core] + swap_in[phase, chunk]).astype(BF16)

        def relay(targets):
            for target in targets:
                remote(p_out.at[phase, chunk], relay_in.at[phase, chunk, row], r_send.at[phase], r_recv.at[phase, chunk], target)

        @pl.when(phase < top)
        def _():
            relay(ahead_ids)

        @pl.when(phase > ticks)
        def _():
            relay(behind_ids)

        @pl.when(lax.rem(chunk, per_row) == per_row - 1)
        def _():
            holder = lax.div(chunk, per_row)
            ready = p_out.at[phase, pl.ds(holder * per_row, per_row)]

            @pl.when(row == holder)
            def _():
                own_in[phase, row] = ready[...]

            @pl.when(row != holder)
            def _():
                remote(ready, own_in.at[phase, row], o_send.at[phase], o_recv.at[phase], {"row": holder})

    def joined(ref):
        low = ref[0].astype(F32) + ref[2].astype(F32)
        high = ref[1].astype(F32) + ref[3].astype(F32)
        return jnp.concatenate([low, high], axis=1)

    def enter_forward(tick, chunk):
        phase = tick - 1
        await_bytes(relay_in.at[phase, chunk], r_recv.at[phase, chunk])
        here = base[tick - 1, span(chunk * size, size), :]
        rebuilt = (here.astype(F32) + joined(relay_in.at[phase, chunk])).astype(BF16)
        xs[chunk_rows(tick, chunk), :] = jnp.where(section == 0, here, rebuilt)

    def enter_back(tick, chunk):
        phase = ticks + tick + 1
        await_bytes(relay_in.at[phase, chunk], r_recv.at[phase, chunk])
        here = late[tick, span(chunk * size, size), :]
        arrived = joined(relay_in.at[phase, chunk]).astype(BF16)
        gs[chunk_rows(tick, chunk), :] = jnp.where(last, here, arrived)

    def own_sum(phase):
        await_bytes(own_in.at[phase, pl.ds(0, n_row - 1)], o_recv.at[phase])
        return jnp.concatenate([joined(own_in.at[phase, :, piece]) for piece in range(per_row)], axis=0)

    def turn_weights(block, carry):
        hidden_block = span(block * width, width)
        up_t[hidden_block, :] = w_up[:, hidden_block].T
        down_t[:, hidden_block] = w_down[hidden_block, :].T
        return carry

    lax.fori_loop(0, w_up.shape[1] // width, turn_weights, 0)
    await_bytes(xs.at[pl.ds(0, (n_row - 1) * rows)], pre_recv.at[0])
    rounds = 2 * ticks - 1

    def when(condition):
        return pl.when(condition)

    def place_of(step, offset):
        time = step - offset
        turn = lax.div(time, PERIOD)
        inside = lax.rem(time, PERIOD)
        chunk = lax.div(inside, STRIDE)
        due = jnp.logical_and(chunk < chunks, lax.rem(inside, STRIDE) == 0)
        valid = jnp.logical_and(time >= 0, jnp.logical_and(due, turn < rounds))
        return turn, jnp.minimum(chunk, chunks - 1), valid

    def side_of(step, offset, every):
        time = step - offset
        chunk = lax.div(time, every)
        due = jnp.logical_and(time >= 0, jnp.logical_and(chunk < chunks, lax.rem(time, every) == 0))
        return jnp.minimum(chunk, chunks - 1), due

    back_top = ticks + top

    def phase_of(turn, switch):
        return jnp.where(turn < switch, turn, ticks + 2 * top - turn)

    def body(step, carry):
        turn, chunk, valid = place_of(step, AT_HAND)
        spare, spare_due = side_of(step, SPARE_START + AT_HAND - AT_ACTIVATE, SPARE_EVERY)

        @when(valid)
        def _():
            hand_on(phase_of(turn, top), chunk)

        @when(spare_due)
        def _():
            hand_on(top, spare)

        turn, chunk, valid = place_of(step, AT_CONTRACT)
        spare, spare_due = side_of(step, SPARE_START + AT_CONTRACT - AT_ACTIVATE, SPARE_EVERY)

        @when(jnp.logical_and(valid, turn < top))
        def _():
            contract_forward(turn, chunk)

        @when(jnp.logical_and(valid, turn >= top))
        def _():
            contract_back(2 * top - turn, chunk)

        @when(spare_due)
        def _():
            contract_forward(top, spare)

        @when(jnp.logical_or(rank == 1, rank == 2))
        def _():
            turn, chunk, valid = place_of(step, AT_FORWARD)
            spare, spare_due = side_of(step, SPARE_START + AT_FORWARD - AT_ACTIVATE, SPARE_EVERY)

            @when(jnp.logical_and(valid, turn < top))
            def _():
                forward(turn, turn, chunk, act)

            @when(jnp.logical_and(valid, turn >= top))
            def _():
                forward(ticks + 2 * top - turn, 2 * top - turn, chunk, gpre)

            @when(spare_due)
            def _():
                forward(top, top, spare, act)

            turn, chunk, valid = place_of(step, AT_COMBINE)
            early, early_due = side_of(step, EARLY_START + AT_COMBINE, EARLY_EVERY)

            @when(valid)
            def _():
                combine(phase_of(turn, ticks), chunk)

            @when(early_due)
            def _():
                combine(back_top, early)

        @when(rank == 0)
        def _():
            turn, chunk, valid = place_of(step, AT_ACTIVATE)
            spare, spare_due = side_of(step, SPARE_START, SPARE_EVERY)

            @when(jnp.logical_and(valid, turn <= top))
            def _():
                activate(turn, chunk)

            @when(jnp.logical_and(valid, turn < top))
            def _():
                spread(turn, turn, chunk, act)

            @when(jnp.logical_and(valid, turn >= top))
            def _():
                differentiate(2 * top - turn, chunk)

            @when(spare_due)
            def _():
                spread(top, top, spare, act)

            turn, chunk, valid = place_of(step, AT_GATHER)
            early, early_due = side_of(step, EARLY_START + AT_GATHER, EARLY_EVERY)

            @when(valid)
            def _():
                gather(phase_of(turn, ticks), chunk)

            @when(early_due)
            def _():
                gather(back_top, early)

        e_turn, e_chunk, e_valid = place_of(step, 0)
        early, early_due = side_of(step, EARLY_START, EARLY_EVERY)

        @when(jnp.logical_and(e_valid, e_turn <= top))
        def _():
            @when(e_turn > 0)
            def _():
                enter_forward(e_turn, e_chunk)

            expand_forward(e_turn, e_chunk)

        @when(jnp.logical_and(e_valid, e_turn > top))
        def _():
            enter_back(2 * top - e_turn, e_chunk)
            expand_back(2 * top - e_turn, e_chunk)

        @when(early_due)
        def _():
            expand_back(top, early)

        @when(step == EARLY_START - 1)
        def _():
            await_bytes(gs.at[pl.ds(0, (n_row - 1) * rows)], pre_recv.at[1])
            await_bytes(base.at[:, pl.ds(0, (n_row - 1) * rows)], pre_recv.at[2])

            @when(last)
            def _():
                await_bytes(late.at[:, pl.ds(0, (n_row - 1) * rows)], pre_recv.at[3])

        return carry

    lax.fori_loop(0, (rounds - 1) * PERIOD + chunks * STRIDE + AT_HAND, body, 0)

    contract_first = (((0,), (0,)), ((), ()))
    for side in range(2):
        columns = pl.ds(side * wide, wide)
        grad_up[:, columns] = lax.dot_general(xs[...], gpre[side], contract_first, preferred_element_type=F32).astype(BF16)
        grad_down[columns, :] = lax.dot_general(act[side], gs[...], contract_first, preferred_element_type=F32).astype(BF16)
    for tick in range(ticks):
        sec_in[tick] = xs[own_rows(tick), :]
        sec_out[tick] = (own_sum(tick) + pick(send_base, tick).astype(F32)).astype(BF16)
    for tick in range(top, -1, -1):
        in_grad[tick] = own_sum(ticks + tick).astype(BF16)

    count = (n_row - 1) * rows
    await_bytes(xs.at[pl.ds(0, count)], pre_send.at[0])
    await_bytes(gs.at[pl.ds(0, count)], pre_send.at[1])
    await_bytes(base.at[:, pl.ds(0, count)], pre_send.at[2])

    @pl.when(last)
    def _():
        await_bytes(late.at[:, pl.ds(0, count)], pre_send.at[3])

    for phase in range(phases):
        @pl.when(rank == 0)
        def _(phase=phase):
            await_bytes(b_in.at[phase], b_send.at[phase])
            await_bytes(a_in.at[phase], c_send.at[phase])

        @pl.when(rank > 0)
        def _(phase=phase):
            await_bytes(a_out.at[phase], a_send.at[phase])

        @pl.when(rank == 1)
        def _(phase=phase):
            await_bytes(a_out.at[phase], c_send.at[phase])

        @pl.when(rank == 2)
        def _(phase=phase):
            await_bytes(c_out.at[phase], c_send.at[phase])

        await_bytes(swap_in.at[phase], s_send.at[phase])
        if phase != top and phase != ticks:
            await_bytes(relay_in.at[phase], r_send.at[phase])
        await_bytes(own_in.at[phase, pl.ds(0, n_row - 1)], o_send.at[phase])


def per_device(inputs, sample_ids, send_base, recv_base, w_up, w_down, cotangent):
    ticks, rows, width = inputs.shape[1:]
    n_row = lax.axis_size("row")
    tokens = rows * n_row
    chunks = tokens // SIZE
    hidden = w_up.shape[2]
    wide = hidden // 2
    phases = 2 * ticks
    half = width // 2
    dma = pltpu.SemaphoreType.DMA
    vmem = pl.BlockSpec(memory_space=pltpu.VMEM)
    outs = pl.pallas_call(
        kernel,
        out_shape=[
            jax.ShapeDtypeStruct((ticks, rows, width), BF16),
            jax.ShapeDtypeStruct((ticks, rows, width), BF16),
            jax.ShapeDtypeStruct((ticks, rows, width), BF16),
            jax.ShapeDtypeStruct((width, hidden), BF16),
            jax.ShapeDtypeStruct((hidden, width), BF16),
        ],
        in_specs=[pl.BlockSpec(memory_space=pltpu.SMEM)] + [vmem] * 6,
        out_specs=[vmem] * 5,
        scratch_shapes=[
            pltpu.VMEM((hidden, width), BF16),
            pltpu.VMEM((width, hidden), BF16),
            pltpu.VMEM((ticks * tokens, width), BF16),
            pltpu.VMEM((ticks * tokens, width), BF16),
            pltpu.VMEM((ticks - 1, rows, width), BF16),
            pltpu.VMEM((ticks - 1, tokens, width), BF16),
            pltpu.VMEM((ticks - 1, tokens, width), BF16),
            pltpu.VMEM((2, ticks * tokens, wide), BF16),
            pltpu.VMEM((2, ticks * tokens, wide), BF16),
            pltpu.VMEM((2, ticks * tokens, wide), F32),
            pltpu.VMEM((phases, chunks, 2, SIZE, wide), BF16),
            pltpu.VMEM((phases, chunks, 3, SIZE, wide), BF16),
            pltpu.VMEM((phases, chunks, SIZE, wide), BF16),
            pltpu.VMEM((phases, chunks, 2, SIZE, wide), BF16),
            pltpu.VMEM((phases, chunks, 2, SIZE, wide), BF16),
            pltpu.VMEM((phases, chunks, 2, SIZE, half), F32),
            pltpu.VMEM((phases, chunks, SIZE, half), F32),
            pltpu.VMEM((phases, chunks, SIZE, half), BF16),
            pltpu.VMEM((phases, chunks, n_row, SIZE, half), BF16),
            pltpu.VMEM((phases, n_row, rows // SIZE, SIZE, half), BF16),
            dma((4,)), dma((4,)),
            dma((phases,)), dma((phases, chunks)),
            dma((phases,)), dma((phases, chunks)),
            dma((phases,)), dma((phases, chunks, 2)),
            dma((phases,)), dma((phases, chunks)),
            dma((phases,)), dma((phases, chunks)),
            dma((phases,)), dma((phases,)),
        ],
        compiler_params=pltpu.CompilerParams(
            collective_id=0, has_side_effects=True, vmem_limit_bytes=56 << 20
        ),
    )(sample_ids, inputs[0], send_base[0], recv_base[0], w_up[0], w_down[0], cotangent[0])
    return tuple(value[None] for value in outs)


def solution(mesh):
    pieces = P("section", None, "row", "col")
    ups, downs = P("section", "col", "row"), P("section", "row", "col")
    return jax.shard_map(
        per_device,
        mesh=mesh,
        in_specs=(pieces, P(), pieces, pieces, ups, downs, pieces),
        out_specs=(pieces, pieces, pieces, ups, downs),
        check_vma=False,
    )
```

```python
import jax
import jax.numpy as jnp
from jax import lax
from jax.experimental import pallas as pl
from jax.experimental.pallas import tpu as pltpu
from jax.sharding import PartitionSpec as P

MESH = pl.DeviceIdType.MESH
GROUP = 4
SIZE = 16
PERIOD = 34
STRIDE = 3
AT_COMBINE, AT_GATHER, AT_ACTIVATE, AT_FORWARD, AT_CONTRACT, AT_HAND = 4, 8, 13, 18, 24, 25
EARLY_START, EARLY_EVERY = 19, 3
SPARE_START, SPARE_EVERY = 105, 6
F32 = jnp.float32
BF16 = jnp.bfloat16


def kernel(
    ids, inputs, send_base, recv_base, w_up, w_down, cotangent,
    sec_in, sec_out, in_grad, grad_up, grad_down,
    up_t, down_t, xs, gs, stage, base, late, act, gpre, pre,
    a_out, a_in, c_out, b_out, b_in, part, swap_in, p_out, relay_in, own_in,
    pre_send, pre_recv, a_send, a_recv, b_send, b_recv, c_send, c_recv,
    s_send, s_recv, r_send, r_recv, o_send, o_recv,
):
    ticks, rows, width = inputs.shape
    tokens = xs.shape[0] // ticks
    chunks, size, wide = a_out.shape[1], a_out.shape[3], a_out.shape[4]
    per_row = rows // size
    half = width // 2
    top = ticks - 1
    phases = 2 * ticks
    section, row, col = (lax.axis_index(n) for n in ("section", "row", "col"))
    sections, n_row, n_col = (lax.axis_size(n) for n in ("section", "row", "col"))
    core = lax.rem(row, 2)
    place = lax.rem(col, GROUP)
    first = col - place
    rank = jnp.where(first == 0, GROUP - 1 - place, place)

    def at_rank(number):
        return {"col": first + jnp.where(first == 0, GROUP - 1 - number, number)}

    mates = [{"col": first + lax.rem(place + d, GROUP)} for d in range(1, GROUP)]
    across = {"col": n_col - 1 - col}
    peers = [{"row": lax.rem(row + d, n_row)} for d in range(1, n_row)]
    twin = {"row": row + 1 - 2 * core}
    ahead = lax.rem(section + 1, sections)
    behind = lax.rem(section + sections - 1, sections)
    ahead_ids = [{"section": ahead, "row": lax.rem(row + d, n_row)} for d in range(n_row)]
    behind_ids = [{"section": behind, "row": lax.rem(row + d, n_row)} for d in range(n_row)]

    def remote(src, dst, send_sem, recv_sem, where):
        pltpu.make_async_remote_copy(
            src_ref=src, dst_ref=dst, send_sem=send_sem, recv_sem=recv_sem,
            device_id=where, device_id_type=MESH,
        ).start()

    def await_bytes(ref, sem):
        pltpu.make_async_copy(ref, ref, sem).wait()

    def span(start, count):
        return pl.ds(pl.multiple_of(start, count), count)

    def chunk_rows(tick, chunk):
        return span(tick * tokens + chunk * size, size)

    def own_rows(tick):
        return span(tick * tokens + row * rows, rows)

    def pick(table, tick):
        return table[ids[tick - section + sections - 1]]

    barrier = pltpu.get_barrier_semaphore()
    friends = mates + [across] + peers + ahead_ids + behind_ids
    for friend in friends:
        pl.semaphore_signal(barrier, inc=1, device_id=friend, device_id_type=MESH)
    pl.semaphore_wait(barrier, len(friends))

    last = section == sections - 1
    for peer in peers:
        remote(inputs.at[0], xs.at[own_rows(0)], pre_send.at[0], pre_recv.at[0], peer)
    for tick in range(1, ticks):
        stage[tick - 1] = jnp.where(section == 0, inputs[tick], pick(recv_base, tick))
    for peer in peers:
        remote(cotangent.at[top], gs.at[own_rows(top)], pre_send.at[1], pre_recv.at[1], peer)
    for peer in peers:
        for tick in range(1, ticks):
            remote(stage.at[tick - 1], base.at[tick - 1, span(row * rows, rows)], pre_send.at[2], pre_recv.at[2], peer)

    @pl.when(last)
    def _():
        for peer in peers:
            for tick in range(top):
                remote(cotangent.at[tick], late.at[tick, span(row * rows, rows)], pre_send.at[3], pre_recv.at[3], peer)

    xs[own_rows(0), :] = inputs[0]
    gs[own_rows(top), :] = cotangent[top]
    for tick in range(1, ticks):
        base[tick - 1, span(row * rows, rows), :] = stage[tick - 1]
    for tick in range(top):
        late[tick, span(row * rows, rows), :] = cotangent[tick]

    early_half = jnp.where(rank >= 2, 1, 0)
    early_to = at_rank(jnp.where(rank == 1, 0, 1))
    early_slot = jnp.where(rank == 3, 0, 1)

    def expand(phase, chunk, value, product):
        def compute(side):
            a_out[phase, chunk, side] = product(value, span(side * wide, wide)).astype(BF16)

        compute(early_half)

        @pl.when(rank > 0)
        def _():
            remote(a_out.at[phase, chunk, early_half], a_in.at[phase, chunk, early_slot], a_send.at[phase], a_recv.at[phase, chunk], early_to)

        compute(1 - early_half)

        @pl.when(rank == 3)
        def _():
            remote(a_out.at[phase, chunk, 0], a_in.at[phase, chunk, 0], a_send.at[phase], a_recv.at[phase, chunk], at_rank(2))

    def expand_forward(tick, chunk):
        def product(value, columns):
            return jnp.dot(value, w_up[:, columns], preferred_element_type=F32)

        expand(tick, chunk, xs[chunk_rows(tick, chunk), :], product)

    def expand_back(tick, chunk):
        def product(value, columns):
            return jnp.dot(value, down_t[:, columns], preferred_element_type=F32)

        expand(ticks + tick, chunk, gs[chunk_rows(tick, chunk), :], product)

    def partial_sum(phase, chunk, side, slots):
        total = a_out[phase, chunk, side].astype(F32)
        for slot in slots:
            total = total + a_in[phase, chunk, slot].astype(F32)
        return total.astype(BF16)

    def combine(phase, chunk):
        def pass_on(side, slots, slot):
            await_bytes(a_in.at[phase, chunk, pl.ds(0, slots)], a_recv.at[phase, chunk])
            c_out[phase, chunk] = partial_sum(phase, chunk, side, range(slots))
            remote(c_out.at[phase, chunk], a_in.at[phase, chunk, slot], a_send.at[phase], a_recv.at[phase, chunk], at_rank(0))

        @pl.when(rank == 2)
        def _():
            pass_on(0, 1, 0)

        @pl.when(rank == 1)
        def _():
            pass_on(1, 2, 2)

    def gather(phase, chunk):
        await_bytes(a_in.at[phase, chunk], a_recv.at[phase, chunk])
        b_out[phase, chunk, 0] = partial_sum(phase, chunk, 0, (0, 1))
        b_out[phase, chunk, 1] = partial_sum(phase, chunk, 1, (2,))
        remote(b_out.at[phase, chunk], b_in.at[phase, chunk], b_send.at[phase], b_recv.at[phase, chunk], across)

    def summed(phase, chunk):
        await_bytes(b_in.at[phase, chunk], b_recv.at[phase, chunk])
        return b_out[phase, chunk].astype(F32) + b_in[phase, chunk].astype(F32)

    def spread(phase, tick, chunk, hidden):
        def send(side, number):
            ref = hidden.at[side, chunk_rows(tick, chunk)]
            remote(ref, ref, c_send.at[phase], c_recv.at[phase, chunk, side], at_rank(number))

        send(1, 1)
        send(0, 2)
        send(0, 1)

    def forward(phase, tick, chunk, hidden):
        def pass_on(side, numbers):
            ref = hidden.at[side, chunk_rows(tick, chunk)]
            await_bytes(ref, c_recv.at[phase, chunk, side])
            for number in numbers:
                remote(ref, ref, c_send.at[phase], c_recv.at[phase, chunk, side], at_rank(number))

        @pl.when(rank == 1)
        def _():
            pass_on(1, (3, 2))

        @pl.when(rank == 2)
        def _():
            pass_on(0, (3,))

    def activate(tick, chunk):
        value = summed(tick, chunk)
        pre[:, chunk_rows(tick, chunk), :] = value
        act[:, chunk_rows(tick, chunk), :] = (value / (1.0 + jnp.exp(-value))).astype(BF16)

    def differentiate(tick, chunk):
        value = pre[:, chunk_rows(tick, chunk), :]
        sig = 1.0 / (1.0 + jnp.exp(-value))
        slope = sig * (1.0 + value * (1.0 - sig))
        gpre[:, chunk_rows(tick, chunk), :] = (summed(ticks + tick, chunk) * slope).astype(BF16)
        spread(ticks + tick, tick, chunk, gpre)

    def await_hidden(phase, tick, chunk, hidden):
        for side, known in ((0, 2), (1, 1)):
            @pl.when(jnp.logical_and(rank != 0, rank != known))
            def _(side=side):
                await_bytes(hidden.at[side, chunk_rows(tick, chunk)], c_recv.at[phase, chunk, side])

    def swap(phase, chunk, total, skip):
        def halves(value):
            return value[:, :half], value[:, half:]

        part[phase, chunk, 0], part[phase, chunk, 1] = halves(total)

        @pl.when(row == lax.div(chunk, per_row))
        def _():
            part[phase, chunk, 0], part[phase, chunk, 1] = halves(total + skip())

        remote(part.at[phase, chunk, 1 - core], swap_in.at[phase, chunk], s_send.at[phase], s_recv.at[phase, chunk], twin)

    def contract_forward(tick, chunk):
        await_hidden(tick, tick, chunk, act)
        total = 0.0
        for side in range(2):
            total = total + jnp.dot(act[side, chunk_rows(tick, chunk), :], w_down[pl.ds(side * wide, wide), :], preferred_element_type=F32)

        def skip():
            sample = ids[tick - section + sections - 1]
            stored = send_base[sample, span(lax.rem(chunk, per_row) * size, size), :]
            return xs[chunk_rows(tick, chunk), :].astype(F32) - stored.astype(F32)

        swap(tick, chunk, total, skip)

    def contract_back(tick, chunk):
        await_hidden(ticks + tick, tick, chunk, gpre)
        total = 0.0
        for side in range(2):
            total = total + jnp.dot(gpre[side, chunk_rows(tick, chunk), :], up_t[pl.ds(side * wide, wide), :], preferred_element_type=F32)
        swap(ticks + tick, chunk, total, lambda: gs[chunk_rows(tick, chunk), :].astype(F32))

    def hand_on(phase, chunk):
        await_bytes(swap_in.at[phase, chunk], s_recv.at[phase, chunk])
        p_out[phase, chunk] = (part[phase, chunk, core] + swap_in[phase, chunk]).astype(BF16)

        def relay(targets):
            for target in targets[2:] + targets[:2]:
                remote(p_out.at[phase, chunk], relay_in.at[phase, chunk, row], r_send.at[phase], r_recv.at[phase, chunk], target)

        @pl.when(phase < top)
        def _():
            relay(ahead_ids)

        @pl.when(phase > ticks)
        def _():
            relay(behind_ids)

        @pl.when(lax.rem(chunk, per_row) == per_row - 1)
        def _():
            holder = lax.div(chunk, per_row)
            ready = p_out.at[phase, pl.ds(holder * per_row, per_row)]

            @pl.when(row == holder)
            def _():
                own_in[phase, row] = ready[...]

            @pl.when(row != holder)
            def _():
                remote(ready, own_in.at[phase, row], o_send.at[phase], o_recv.at[phase], {"row": holder})

    def joined(ref):
        low = ref[0].astype(F32) + ref[2].astype(F32)
        high = ref[1].astype(F32) + ref[3].astype(F32)
        return jnp.concatenate([low, high], axis=1)

    def enter_forward(tick, chunk):
        phase = tick - 1
        await_bytes(relay_in.at[phase, chunk], r_recv.at[phase, chunk])
        here = base[tick - 1, span(chunk * size, size), :]
        rebuilt = (here.astype(F32) + joined(relay_in.at[phase, chunk])).astype(BF16)
        xs[chunk_rows(tick, chunk), :] = jnp.where(section == 0, here, rebuilt)

    def enter_back(tick, chunk):
        phase = ticks + tick + 1
        await_bytes(relay_in.at[phase, chunk], r_recv.at[phase, chunk])
        here = late[tick, span(chunk * size, size), :]
        arrived = joined(relay_in.at[phase, chunk]).astype(BF16)
        gs[chunk_rows(tick, chunk), :] = jnp.where(last, here, arrived)

    def own_sum(phase):
        await_bytes(own_in.at[phase, pl.ds(0, n_row - 1)], o_recv.at[phase])
        return jnp.concatenate([joined(own_in.at[phase, :, piece]) for piece in range(per_row)], axis=0)

    def turn_weights(block, carry):
        hidden_block = span(block * width, width)
        up_t[hidden_block, :] = w_up[:, hidden_block].T
        down_t[:, hidden_block] = w_down[hidden_block, :].T
        return carry

    lax.fori_loop(0, w_up.shape[1] // width, turn_weights, 0)
    await_bytes(xs.at[pl.ds(0, (n_row - 1) * rows)], pre_recv.at[0])
    rounds = 2 * ticks - 1

    def when(condition):
        return pl.when(condition)

    def place_of(step, offset):
        time = step - offset
        turn = lax.div(time, PERIOD)
        inside = lax.rem(time, PERIOD)
        chunk = lax.div(inside, STRIDE)
        due = jnp.logical_and(chunk < chunks, lax.rem(inside, STRIDE) == 0)
        valid = jnp.logical_and(time >= 0, jnp.logical_and(due, turn < rounds))
        return turn, jnp.minimum(chunk, chunks - 1), valid

    def side_of(step, offset, every):
        time = step - offset
        chunk = lax.div(time, every)
        due = jnp.logical_and(time >= 0, jnp.logical_and(chunk < chunks, lax.rem(time, every) == 0))
        return jnp.minimum(chunk, chunks - 1), due

    back_top = ticks + top

    def phase_of(turn, switch):
        return jnp.where(turn < switch, turn, ticks + 2 * top - turn)

    def body(step, carry):
        turn, chunk, valid = place_of(step, AT_HAND)
        spare, spare_due = side_of(step, SPARE_START + AT_HAND - AT_ACTIVATE, SPARE_EVERY)

        @when(valid)
        def _():
            hand_on(phase_of(turn, top), chunk)

        @when(spare_due)
        def _():
            hand_on(top, spare)

        turn, chunk, valid = place_of(step, AT_CONTRACT)
        spare, spare_due = side_of(step, SPARE_START + AT_CONTRACT - AT_ACTIVATE, SPARE_EVERY)

        @when(jnp.logical_and(valid, turn < top))
        def _():
            contract_forward(turn, chunk)

        @when(jnp.logical_and(valid, turn >= top))
        def _():
            contract_back(2 * top - turn, chunk)

        @when(spare_due)
        def _():
            contract_forward(top, spare)

        @when(jnp.logical_or(rank == 1, rank == 2))
        def _():
            turn, chunk, valid = place_of(step, AT_FORWARD)
            spare, spare_due = side_of(step, SPARE_START + AT_FORWARD - AT_ACTIVATE, SPARE_EVERY)

            @when(jnp.logical_and(valid, turn < top))
            def _():
                forward(turn, turn, chunk, act)

            @when(jnp.logical_and(valid, turn >= top))
            def _():
                forward(ticks + 2 * top - turn, 2 * top - turn, chunk, gpre)

            @when(spare_due)
            def _():
                forward(top, top, spare, act)

            turn, chunk, valid = place_of(step, AT_COMBINE)
            early, early_due = side_of(step, EARLY_START + AT_COMBINE, EARLY_EVERY)

            @when(valid)
            def _():
                combine(phase_of(turn, ticks), chunk)

            @when(early_due)
            def _():
                combine(back_top, early)

        @when(rank == 0)
        def _():
            turn, chunk, valid = place_of(step, AT_ACTIVATE)
            spare, spare_due = side_of(step, SPARE_START, SPARE_EVERY)

            @when(jnp.logical_and(valid, turn <= top))
            def _():
                activate(turn, chunk)

            @when(jnp.logical_and(valid, turn < top))
            def _():
                spread(turn, turn, chunk, act)

            @when(jnp.logical_and(valid, turn >= top))
            def _():
                differentiate(2 * top - turn, chunk)

            @when(spare_due)
            def _():
                spread(top, top, spare, act)

            turn, chunk, valid = place_of(step, AT_GATHER)
            early, early_due = side_of(step, EARLY_START + AT_GATHER, EARLY_EVERY)

            @when(valid)
            def _():
                gather(phase_of(turn, ticks), chunk)

            @when(early_due)
            def _():
                gather(back_top, early)

        e_turn, e_chunk, e_valid = place_of(step, 0)
        early, early_due = side_of(step, EARLY_START, EARLY_EVERY)

        @when(jnp.logical_and(e_valid, e_turn <= top))
        def _():
            @when(e_turn > 0)
            def _():
                enter_forward(e_turn, e_chunk)

            expand_forward(e_turn, e_chunk)

        @when(jnp.logical_and(e_valid, e_turn > top))
        def _():
            enter_back(2 * top - e_turn, e_chunk)
            expand_back(2 * top - e_turn, e_chunk)

        @when(early_due)
        def _():
            expand_back(top, early)

        @when(step == EARLY_START - 1)
        def _():
            await_bytes(gs.at[pl.ds(0, (n_row - 1) * rows)], pre_recv.at[1])
            await_bytes(base.at[:, pl.ds(0, (n_row - 1) * rows)], pre_recv.at[2])

            @when(last)
            def _():
                await_bytes(late.at[:, pl.ds(0, (n_row - 1) * rows)], pre_recv.at[3])

        return carry

    lax.fori_loop(0, (rounds - 1) * PERIOD + chunks * STRIDE + AT_HAND, body, 0)

    contract_first = (((0,), (0,)), ((), ()))
    for side in range(2):
        columns = pl.ds(side * wide, wide)
        grad_up[:, columns] = lax.dot_general(xs[...], gpre[side], contract_first, preferred_element_type=F32).astype(BF16)
        grad_down[columns, :] = lax.dot_general(act[side], gs[...], contract_first, preferred_element_type=F32).astype(BF16)
    for tick in range(ticks):
        sec_in[tick] = xs[own_rows(tick), :]
        sec_out[tick] = (own_sum(tick) + pick(send_base, tick).astype(F32)).astype(BF16)
    for tick in range(top, -1, -1):
        in_grad[tick] = own_sum(ticks + tick).astype(BF16)

    count = (n_row - 1) * rows
    await_bytes(xs.at[pl.ds(0, count)], pre_send.at[0])
    await_bytes(gs.at[pl.ds(0, count)], pre_send.at[1])
    await_bytes(base.at[:, pl.ds(0, count)], pre_send.at[2])

    @pl.when(last)
    def _():
        await_bytes(late.at[:, pl.ds(0, count)], pre_send.at[3])

    for phase in range(phases):
        @pl.when(rank == 0)
        def _(phase=phase):
            await_bytes(b_in.at[phase], b_send.at[phase])
            await_bytes(a_in.at[phase], c_send.at[phase])

        @pl.when(rank > 0)
        def _(phase=phase):
            await_bytes(a_out.at[phase], a_send.at[phase])

        @pl.when(rank == 1)
        def _(phase=phase):
            await_bytes(a_out.at[phase], c_send.at[phase])

        @pl.when(rank == 2)
        def _(phase=phase):
            await_bytes(c_out.at[phase], c_send.at[phase])

        await_bytes(swap_in.at[phase], s_send.at[phase])
        if phase != top and phase != ticks:
            await_bytes(relay_in.at[phase], r_send.at[phase])
        await_bytes(own_in.at[phase, pl.ds(0, n_row - 1)], o_send.at[phase])


def per_device(inputs, sample_ids, send_base, recv_base, w_up, w_down, cotangent):
    ticks, rows, width = inputs.shape[1:]
    n_row = lax.axis_size("row")
    tokens = rows * n_row
    chunks = tokens // SIZE
    hidden = w_up.shape[2]
    wide = hidden // 2
    phases = 2 * ticks
    half = width // 2
    dma = pltpu.SemaphoreType.DMA
    vmem = pl.BlockSpec(memory_space=pltpu.VMEM)
    outs = pl.pallas_call(
        kernel,
        out_shape=[
            jax.ShapeDtypeStruct((ticks, rows, width), BF16),
            jax.ShapeDtypeStruct((ticks, rows, width), BF16),
            jax.ShapeDtypeStruct((ticks, rows, width), BF16),
            jax.ShapeDtypeStruct((width, hidden), BF16),
            jax.ShapeDtypeStruct((hidden, width), BF16),
        ],
        in_specs=[pl.BlockSpec(memory_space=pltpu.SMEM)] + [vmem] * 6,
        out_specs=[vmem] * 5,
        scratch_shapes=[
            pltpu.VMEM((hidden, width), BF16),
            pltpu.VMEM((width, hidden), BF16),
            pltpu.VMEM((ticks * tokens, width), BF16),
            pltpu.VMEM((ticks * tokens, width), BF16),
            pltpu.VMEM((ticks - 1, rows, width), BF16),
            pltpu.VMEM((ticks - 1, tokens, width), BF16),
            pltpu.VMEM((ticks - 1, tokens, width), BF16),
            pltpu.VMEM((2, ticks * tokens, wide), BF16),
            pltpu.VMEM((2, ticks * tokens, wide), BF16),
            pltpu.VMEM((2, ticks * tokens, wide), F32),
            pltpu.VMEM((phases, chunks, 2, SIZE, wide), BF16),
            pltpu.VMEM((phases, chunks, 3, SIZE, wide), BF16),
            pltpu.VMEM((phases, chunks, SIZE, wide), BF16),
            pltpu.VMEM((phases, chunks, 2, SIZE, wide), BF16),
            pltpu.VMEM((phases, chunks, 2, SIZE, wide), BF16),
            pltpu.VMEM((phases, chunks, 2, SIZE, half), F32),
            pltpu.VMEM((phases, chunks, SIZE, half), F32),
            pltpu.VMEM((phases, chunks, SIZE, half), BF16),
            pltpu.VMEM((phases, chunks, n_row, SIZE, half), BF16),
            pltpu.VMEM((phases, n_row, rows // SIZE, SIZE, half), BF16),
            dma((4,)), dma((4,)),
            dma((phases,)), dma((phases, chunks)),
            dma((phases,)), dma((phases, chunks)),
            dma((phases,)), dma((phases, chunks, 2)),
            dma((phases,)), dma((phases, chunks)),
            dma((phases,)), dma((phases, chunks)),
            dma((phases,)), dma((phases,)),
        ],
        compiler_params=pltpu.CompilerParams(
            collective_id=0, has_side_effects=True, vmem_limit_bytes=56 << 20
        ),
    )(sample_ids, inputs[0], send_base[0], recv_base[0], w_up[0], w_down[0], cotangent[0])
    return tuple(value[None] for value in outs)


def solution(mesh):
    pieces = P("section", None, "row", "col")
    ups, downs = P("section", "col", "row"), P("section", "row", "col")
    return jax.shard_map(
        per_device,
        mesh=mesh,
        in_specs=(pieces, P(), pieces, pieces, ups, downs, pieces),
        out_specs=(pieces, pieces, pieces, ups, downs),
        check_vma=False,
    )
```
